1024 devices in a mesh: cluster: 32 (over x, y, core), sample: 32 (over z).
Axes of the slice: x: 4, y: 4, z: 32, core: 2. Of those that a mesh axis runs over, the one named last changes fastest.
Arguments:
- child_pattern: float32 [2, 4096, 16384], P(None, 'cluster', 'sample'), may hold values from -6 to 6
- child_local: float32 [2, 4096, 16384], P(None, 'cluster', 'sample'), may hold values from -6 to 6
- interp_weight: float32 [6, 32768], P(None, 'sample'), may hold values from -0.1 to 0.3
- child_phase: float32 [8, 32768], P(None, 'sample'), may hold values from -3.140625 to 3.140625
- translator: float32 [316, 2, 32768], P(None, None, 'sample'), may hold values from -0.6 to 0.6
- partners: int32 [512, 64], replicated, may hold values from 0 to 511
- operator_id: int32 [512, 64], replicated, may hold values from 0 to 315
- list_len: int32 [512], replicated, may hold values from 8 to 64, as said below
Outputs:
- parent_incoming: float32 [2, 512, 32768], P(None, 'cluster', 'sample')
- child_incoming: float32 [2, 4096, 16384], P(None, 'cluster', 'sample')
The draws below stay inside these ranges and needn't reach their ends.
Inputs may be any that keep to these rules, and one draw needn't show every extreme that they name: Parent q's interaction list is its first list_len[q] entries of partners and operator_id; later entries are unused.
All inputs are finite; a program needn't handle non-finite values.
Results may differ from the reference program's by a relative error of at most 0.0003.
Values sent between devices are 32-bit elements; how exact they have to be, the bound alone decides.
A program may use at most 32 MiB of HBM per device.

```python
import jax
import jax.numpy as jnp
from jax import lax

K1 = 16384
K2 = 32768
TAPS = 6
CHILDREN = 8
NT = 316
LMAX = 64
NP_DEV = 16
NP = 512
NC = 4096


def draw_list_len(key, part):
    key_heavy, key_light, key_long, key_row = jax.random.split(key, 4)
    devices_count = NP // NP_DEV
    heavy_mask = jax.random.randint(key_heavy, (devices_count,), 0, 4) == 0
    heavy_mask = jnp.repeat(heavy_mask, NP_DEV)
    light_len = jax.random.randint(key_light, (NP,), LMAX // 8, LMAX // 4 + 1)
    heavy_len = jax.random.randint(key_long, (NP,), LMAX // 2, LMAX + 1)
    lengths = jnp.where(heavy_mask, heavy_len, light_len)
    forced_row = jax.random.randint(key_row, (), 0, NP)
    return lengths.at[forced_row].set(LMAX).astype(jnp.int32)


def touch_ends(drawn, own_key, low, high):
    extent = drawn.shape
    spot = [jax.random.randint(jax.random.fold_in(own_key, axis), (), 0, extent[axis]) for axis in range(len(extent))]
    drawn = drawn.at[tuple(spot)].set(low)
    longest = extent.index(max(extent))
    spot[longest] = (spot[longest] + 1) % extent[longest]
    return drawn.at[tuple(spot)].set(high)


def levels(own_key, extent, shards, least, largest):
    factor_of, own = 1.0, jax.random.fold_in(own_key, 6)
    for axis_at, blocks in shards:
        heights = jnp.exp(jax.random.uniform(jax.random.fold_in(own, axis_at), (blocks,), jnp.float32, least / len(shards), largest / len(shards)))
        factor_of = factor_of * jnp.repeat(heights, extent[axis_at] // blocks).reshape([-1 if axis == axis_at else 1 for axis in range(len(extent))])
    return factor_of


def gaussian(stream_key, shape, deviation, reach, cuts=(), kind=jnp.bfloat16):
    gain = levels(stream_key, shape, cuts, -0.22, 0.18) if cuts else 1.0
    entries = jax.random.normal(stream_key, shape, jnp.float32) * deviation * gain
    return jnp.minimum(jnp.maximum(entries, -reach), reach).astype(kind)


def setup_inputs(seed: int = 0) -> dict:
    key_of = jax.random.split(jax.random.key(seed), 9)
    child_pattern = gaussian(key_of[0], (2, NC, K1), 1.0, 6.0, ((1, 32), (2, 32)), jnp.float32)
    child_local = gaussian(key_of[1], (2, NC, K1), 1.0, 6.0, ((1, 32), (2, 32)), jnp.float32)
    interp_weight = jnp.clip(-0.1 + 0.4 * jax.random.uniform(key_of[2], (TAPS, K2), jnp.float32) ** levels(key_of[2], (TAPS, K2), ((1, 32),), -0.2, 0.2), -0.1, 0.3)
    child_phase = jnp.clip(jax.random.uniform(key_of[3], (CHILDREN, K2), jnp.float32, -3.140625, 3.140625), -3.140625, 3.140625)
    translator = gaussian(key_of[4], (NT, 2, K2), 0.1, 0.6, ((2, 32),), jnp.float32)
    partners = touch_ends(jax.random.randint(key_of[5], (NP, LMAX), 0, NP), jax.random.fold_in(key_of[5], 1), 0, NP - 1).astype(jnp.int32)
    operator_id = touch_ends(jax.random.randint(key_of[6], (NP, LMAX), 0, NT), jax.random.fold_in(key_of[6], 1), 0, NT - 1).astype(jnp.int32)
    list_len = draw_list_len(jax.random.fold_in(key_of[8], 71), 0)
    return {"child_pattern": child_pattern, "child_local": child_local, "interp_weight": interp_weight, "child_phase": child_phase, "translator": translator, "partners": partners, "operator_id": operator_id, "list_len": list_len}


def upsample_block(children, weight):
    rim_width = TAPS // 2
    base_index = jnp.arange(K2) // 2 - (rim_width - 1)
    total = jnp.zeros((2, children.shape[1], K2), jnp.float32)
    for tap in range(TAPS):
        source_index = ((base_index + tap) % K1).astype(jnp.int32)
        total = total + weight[tap][None, None, :] * jnp.take(children, source_index, axis=2)
    return total


def aggregate(children, weight, cosine, sine):
    upsampled = upsample_block(children, weight).reshape(2, -1, CHILDREN, K2)
    real_part = jnp.sum(cosine[None] * upsampled[0] - sine[None] * upsampled[1], axis=1)
    imag_part = jnp.sum(cosine[None] * upsampled[1] + sine[None] * upsampled[0], axis=1)
    return jnp.stack([real_part, imag_part])


def translate_block(pattern, table, partner_rows, operator_rows, lengths):
    alive_mask = (jnp.arange(LMAX)[None, :] < lengths[:, None]).astype(jnp.float32)
    source = jnp.take(pattern, partner_rows, axis=1)
    coupling = jnp.take(table, operator_rows, axis=0)
    coup_real = coupling[:, :, 0] * alive_mask[:, :, None]
    coup_imag = coupling[:, :, 1] * alive_mask[:, :, None]
    real_part = jnp.sum(coup_real * source[0] - coup_imag * source[1], axis=1)
    imag_part = jnp.sum(coup_real * source[1] + coup_imag * source[0], axis=1)
    return jnp.stack([real_part, imag_part])


def disaggregate(incoming, weight, cosine, sine):
    rim_width = TAPS // 2
    shifted_real = cosine[None] * incoming[0][:, None] + sine[None] * incoming[1][:, None]
    shifted_imag = cosine[None] * incoming[1][:, None] - sine[None] * incoming[0][:, None]
    shifted = jnp.stack([shifted_real, shifted_imag]).reshape(2, -1, K2)
    total = jnp.zeros((2, shifted.shape[1], K1), jnp.float32)
    for tap in range(TAPS):
        paired = (weight[tap][None, None, :] * shifted).reshape(2, shifted.shape[1], K1, 2)
        paired = jnp.sum(paired, axis=3)
        source_index = ((jnp.arange(K1) + rim_width - 1 - tap) % K1).astype(jnp.int32)
        total = total + jnp.take(paired, source_index, axis=2)
    return total


def reference(child_pattern, child_local, interp_weight, child_phase, translator, partners, operator_id, list_len):
    cosine = jnp.cos(child_phase)
    sine = jnp.sin(child_phase)
    blocks = NP // NP_DEV
    grouped = child_pattern.reshape(2, blocks, CHILDREN * NP_DEV, K1).transpose(1, 0, 2, 3)

    def agg_one(children):
        return aggregate(children, interp_weight, cosine, sine)

    parent = lax.map(agg_one, grouped)
    parent = parent.transpose(1, 0, 2, 3).reshape(2, NP, K2)

    def trans_one(item):
        return translate_block(parent, translator, item[0], item[1], item[2])

    rows = (partners.reshape(blocks, NP_DEV, LMAX), operator_id.reshape(blocks, NP_DEV, LMAX), list_len.reshape(blocks, NP_DEV))
    incoming = lax.map(trans_one, rows)
    incoming = incoming.transpose(1, 0, 2, 3).reshape(2, NP, K2)

    def dis_one(block_in):
        return disaggregate(block_in, interp_weight, cosine, sine)

    spread = lax.map(dis_one, incoming.reshape(2, blocks, NP_DEV, K2).transpose(1, 0, 2, 3))
    child_incoming = child_local + spread.transpose(1, 0, 2, 3).reshape(2, NC, K1)
    return incoming, child_incoming
```

```python
import functools

import jax
import jax.numpy as jnp
from jax import lax
from jax.experimental import pallas as pl
from jax.experimental.pallas import tpu as pltpu
from jax.sharding import PartitionSpec as P

TAPS = 6
CHILDREN = 8
PAR = 16
NT = 316
LMAX = 64
MESH = pl.DeviceIdType.MESH
CHUNK_OF = {0: (0, 0), 3: (0, 2), 2: (1, 0), 1: (1, 2)}


def lanes():
    return lax.broadcasted_iota(jnp.int32, (8, 128), 1)


def subs():
    return lax.broadcasted_iota(jnp.int32, (8, 128), 0)


def take(v, index):
    return jnp.take_along_axis(v, index, axis=1)


def split_pairs(v0, v1):
    lane = lanes()
    even = (2 * lane) % 128
    return tuple(
        jnp.where(lane < 64, take(v0, even + odd), take(v1, even + odd)) for odd in (0, 1)
    )


def join_pairs(e, o):
    lane = lanes()
    made = []
    for half in (0, 64):
        at = half + lane // 2
        made.append(jnp.where(lane % 2 == 0, take(e, at), take(o, at)))
    return made


def pack_low(groups):
    lane = lanes()
    total = jnp.zeros((8, 128), jnp.float32)
    for g, v in enumerate(groups):
        total = jnp.where(lane // 4 == g, pltpu.roll(v, 4 * g, 1) if g else v, total)
    return total


def pack_high(groups):
    lane = lanes()
    total = jnp.zeros((8, 128), jnp.float32)
    for g, v in enumerate(groups):
        shift = (4 * g + 4) % 128
        total = jnp.where(lane // 4 == g, pltpu.roll(v, shift, 1) if shift else v, total)
    return total


def as_high_halo(packed, g):
    return pltpu.roll(packed, (128 - 4 * g) % 128, 1) if g else packed


def as_low_halo(packed, g):
    shift = (128 - (4 * g + 4)) % 128
    return pltpu.roll(packed, shift, 1) if shift else packed


def kernel(
    cp, cl, w, ph, t, part, oper, length,
    out0, out1,
    p_0, p_1, ab_0, ab_1, inc_0, inc_1, tv, xpad, clv, wv, phv, wpad, phpad, cs, wb, agg, incpad,
    opv, opm, pidx, oidx, lens,
    halo_out, halo_in, edge_out, edge_in,
    load_sem, index_sem, send_sem, row_sem, col_sem, twin_sem, halo_send, halo_recv, edge_send, edge_recv,
):
    gathered, tables, incoming = (p_0, p_1), (ab_0, ab_1), (inc_0, inc_1)
    me = lax.axis_index("cluster")
    z = lax.axis_index("sample")
    core = me % 2
    y = (me // 2) % 4
    x = me // 8
    step_a = 8 - 6 * core
    step_b = 2 + 6 * core
    at_a = x * (1 - core) + y * core
    at_b = y * (1 - core) + x * core
    twin = me + 1 - 2 * core

    def dev(da, db):
        return step_a * ((at_a + da + 4) % 4) + step_b * ((at_b + db + 4) % 4) + core

    z_low = (z + 31) % 32
    z_high = (z + 1) % 32

    first_row = pl.multiple_of(me * PAR, PAR)
    loads = [
        pltpu.make_async_copy(w, wv, load_sem.at[0]),
        pltpu.make_async_copy(ph, phv, load_sem.at[1]),
        pltpu.make_async_copy(cp, xpad.at[:, :, pl.ds(128, 512)], load_sem.at[2]),
        pltpu.make_async_copy(oper.at[pl.ds(first_row, PAR)], opv, load_sem.at[3]),
        pltpu.make_async_copy(length, lens, load_sem.at[4]),
        pltpu.make_async_copy(part.at[pl.ds(first_row, PAR)], pidx, load_sem.at[5]),
        pltpu.make_async_copy(t, tv, load_sem.at[6]),
        pltpu.make_async_copy(cl, clv, load_sem.at[7]),
    ]
    for load in loads:
        load.start()

    barrier = pltpu.get_barrier_semaphore()
    for there in (dev(1, 0), dev(-1, 0), dev(0, 1), dev(0, -1), twin):
        pl.semaphore_signal(barrier, inc=1, device_id={"cluster": there}, device_id_type=MESH)
    for there in (z_low, z_high):
        pl.semaphore_signal(barrier, inc=1, device_id={"sample": there}, device_id_type=MESH)

    loads[0].wait()
    loads[1].wait()
    for b in range(4):
        main = pl.ds(128 * (b + 1), 128)
        halves = []
        for k in (2 * b, 2 * b + 1):
            halves.append(
                jnp.concatenate([wv[:, 128 * k : 128 * (k + 1)], jnp.zeros((2, 128), jnp.float32)], 0)
            )
        for odd, v in enumerate(split_pairs(*halves)):
            wpad[odd, :, main] = v
        for odd, v in enumerate(
            split_pairs(
                phv[:, 256 * b : 256 * b + 128],
                phv[:, 256 * b + 128 : 256 * b + 256],
            )
        ):
            phpad[odd, :, main] = v

    loads[2].wait()

    def ends(block, packer):
        here = pl.ds(128 * (block + 1), 128)
        children = [xpad[c, 8 * p : 8 * p + 8, here] for c in range(2) for p in range(PAR)]
        others = [wpad[0, :, here], wpad[1, :, here], phpad[0, :, here], phpad[1, :, here]]
        return packer(children), packer(others)

    halo_out[0, 0], halo_out[0, 1] = ends(0, pack_low)
    halo_out[1, 0], halo_out[1, 1] = ends(3, pack_high)
    pl.semaphore_wait(barrier, 7)
    halos = [
        pltpu.make_async_remote_copy(
            src_ref=halo_out.at[side],
            dst_ref=halo_in.at[side],
            send_sem=halo_send.at[side],
            recv_sem=halo_recv.at[side],
            device_id={"sample": there},
            device_id_type=MESH,
        )
        for side, there in ((0, z_low), (1, z_high))
    ]
    for halo in halos:
        halo.start()

    for odd in range(2):
        cs[0, odd, :, 128:640] = jnp.cos(phpad[odd, :, 128:640])
        cs[1, odd, :, 128:640] = jnp.sin(phpad[odd, :, 128:640])

    def broadcast_weights(blocks):
        for odd in range(2):
            for tap in range(TAPS):
                for blk in blocks:
                    here = pl.ds(128 * blk, 128)
                    wb[odd, tap, :, here] = jnp.broadcast_to(wpad[odd, tap : tap + 1, here], (8, 128))

    broadcast_weights(range(1, 5))

    def aggregate(b):
        main = pl.ds(128 * (b + 1), 128)
        weight = [[wb[odd, tap, :, main] for tap in range(TAPS)] for odd in range(2)]
        cosine = [cs[0, odd, :, main] for odd in range(2)]
        sine = [cs[1, odd, :, main] for odd in range(2)]

        def one(p, _):
            rows = pl.ds(pl.multiple_of(8 * p, 8), 8)
            up = []
            for c in range(2):
                wide = xpad[c, rows, pl.ds(128 * b, 384)]
                window = [wide[:, 126 + tap : 254 + tap] for tap in range(TAPS)]
                up.append(
                    [sum(weight[odd][tap] * window[tap] for tap in range(TAPS)) for odd in range(2)]
                )
            for odd in range(2):
                real = cosine[odd] * up[0][odd] - sine[odd] * up[1][odd]
                imag = cosine[odd] * up[1][odd] + sine[odd] * up[0][odd]
                agg[b, odd, 0, pl.ds(p, 1), :] = jnp.sum(real, axis=0, keepdims=True)
                agg[b, odd, 1, pl.ds(p, 1), :] = jnp.sum(imag, axis=0, keepdims=True)
            return 0

        lax.fori_loop(0, PAR, one, 0)
        chunk, place = CHUNK_OF[b]
        for c in range(2):
            for i in range(2):
                pieces = [agg[b, odd, c, 8 * i : 8 * i + 8, :] for odd in range(2)]
                for half, v in enumerate(join_pairs(*pieces)):
                    gathered[chunk][pl.ds(me * PAR + 8 * i, 8), 2 * (place + half) + c, :] = v

    def block(h, d):
        return gathered[h].at[pl.ds(d * PAR, PAR)]

    def send(h, d, target, arrived):
        pltpu.make_async_remote_copy(
            src_ref=block(h, d),
            dst_ref=block(h, d),
            send_sem=send_sem.at[h],
            recv_sem=arrived,
            device_id={"cluster": target},
            device_id_type=MESH,
        ).start()

    def arrive(h, d, arrived):
        pltpu.make_async_remote_copy(
            src_ref=block(h, d),
            dst_ref=block(h, d),
            send_sem=send_sem.at[h],
            recv_sem=arrived,
            device_id={"cluster": twin},
            device_id_type=MESH,
        ).wait_recv()

    def give_twin(h, d):
        send(h, d, twin, twin_sem.at[h])

    OFF = (0, -1, 1, 2)

    def spread_b(h, g):
        d = dev(OFF[g], 0)
        send(h, d, dev(0, 1), col_sem.at[h, g, 0])
        send(h, d, dev(0, -1), col_sem.at[h, g, 1])

    def own(h):
        send(h, me, dev(1, 0), row_sem.at[h, 0])
        send(h, me, dev(-1, 0), row_sem.at[h, 1])
        spread_b(h, 0)
        give_twin(h, me)

    def row_events(h):
        for side, da in ((0, -1), (1, 1)):
            arrive(h, dev(da, 0), row_sem.at[h, side])
            if side == h:
                send(h, dev(da, 0), dev(-da, 0), row_sem.at[h, 2])
            spread_b(h, 1 + side)
            give_twin(h, dev(da, 0))

    def row_far(h):
        arrive(h, dev(2, 0), row_sem.at[h, 2])
        spread_b(h, 3)
        give_twin(h, dev(2, 0))

    def col_near(h, g):
        for side, db in ((0, -1), (1, 1)):
            d = dev(OFF[g], db)
            arrive(h, d, col_sem.at[h, g, side])
            if side == h:
                send(h, d, dev(0, -db), col_sem.at[h, g, 2])
            give_twin(h, d)

    def col_far(h, g):
        d = dev(OFF[g], 2)
        arrive(h, d, col_sem.at[h, g, 2])
        give_twin(h, d)

    def twin_all(h):
        half = gathered[h].at[pl.ds(0, 256)]
        pltpu.make_async_remote_copy(
            src_ref=half, dst_ref=half, send_sem=send_sem.at[h], recv_sem=twin_sem.at[h],
            device_id={"cluster": twin}, device_id_type=MESH,
        ).wait_recv()

    def sent_all(h):
        most = gathered[h].at[pl.ds(0, 31 * PAR)]
        pltpu.make_async_remote_copy(
            src_ref=most, dst_ref=most, send_sem=send_sem.at[h], recv_sem=twin_sem.at[h],
            device_id={"cluster": twin}, device_id_type=MESH,
        ).wait_send()

    def prepare_table(start, stop):
        def one(o, _):
            sub = subs()
            t0 = tv[o, 0:8, :]
            t1 = tv[o, 8:16, :]
            for ab, v in ((ab_0, jnp.where(sub < 4, t0, t1)), (ab_1, jnp.where(sub < 4, t1, t0))):
                ab[o, 0:8, :] = jnp.where(sub % 2 == 0, v, pltpu.roll(v, 1, 0))
                ab[o, 8:16, :] = jnp.where(sub % 2 == 0, pltpu.roll(v, 7, 0), -v)
            return 0

        lax.fori_loop(start, stop, one, 0)

    def translate(h, start, stop):
        def one(q, _):
            first = [jnp.zeros((8, 128), jnp.float32) for _ in range(2)]
            second = [jnp.zeros((8, 128), jnp.float32) for _ in range(2)]
            for slot in range(LMAX):
                source = gathered[h][pidx[q, slot]]
                o = oidx[q, slot]
                first[slot % 2] += tables[h][o, 0:8, :] * source
                second[slot % 2] += tables[h][o, 8:16, :] * source
            cross = second[0] + second[1]
            swapped = jnp.where(subs() % 2 == 0, pltpu.roll(cross, 7, 0), pltpu.roll(cross, 1, 0))
            incoming[h][pl.ds(pl.multiple_of(8 * q, 8), 8), :] = first[0] + first[1] + swapped
            return 0

        lax.fori_loop(start, stop, one, 0)

    def take_out(h):
        for b in range(4):
            chunk, place = CHUNK_OF[b]
            if chunk != h:
                continue
            for c in range(2):
                for i in range(2):
                    pieces = []
                    for half in range(2):
                        v = incoming[h][pl.ds(64 * i + 2 * (place + half) + c, 8, stride=8), :]
                        out0[c, 8 * i : 8 * i + 8, pl.ds(128 * (2 * b + half), 128)] = v
                        pieces.append(v)
                    for odd, v in enumerate(split_pairs(*pieces)):
                        incpad[b + 1, odd, c, 8 * i : 8 * i + 8, :] = v

    GROUPS = [(odd, c, i) for odd in range(2) for c in range(2) for i in range(2)]

    aggregate(2)
    aggregate(1)
    own(1)
    loads[3].wait()
    loads[4].wait()
    live = jnp.zeros((PAR, LMAX), jnp.int32)
    row = lax.broadcasted_iota(jnp.int32, (PAR, LMAX), 0)
    for i in range(PAR):
        live = jnp.where(row == i, lens[me * PAR + i], live)
    slot = lax.broadcasted_iota(jnp.int32, (PAR, LMAX), 1)
    opm[...] = jnp.where(slot < live, opv[...], NT)
    to_smem = pltpu.make_async_copy(opm, oidx, index_sem)
    to_smem.start()

    for halo in halos:
        halo.wait_recv()
    for c in range(2):
        for p in range(PAR):
            g = PAR * c + p
            xpad[c, 8 * p : 8 * p + 8, 640:768] = as_high_halo(halo_in[0, 0], g)
            xpad[c, 8 * p : 8 * p + 8, 0:128] = as_low_halo(halo_in[1, 0], g)
    aggregate(0)
    aggregate(3)
    own(0)

    for g, padded in enumerate((wpad, wpad, phpad, phpad)):
        padded[g % 2, :, 640:768] = as_high_halo(halo_in[0, 1], g)
        padded[g % 2, :, 0:128] = as_low_halo(halo_in[1, 1], g)
    for odd in range(2):
        for here in (slice(0, 128), slice(640, 768)):
            cs[0, odd, :, here] = jnp.cos(phpad[odd, :, here])
            cs[1, odd, :, here] = jnp.sin(phpad[odd, :, here])
    broadcast_weights((0, 5))

    for ab in tables:
        ab[NT] = jnp.zeros((16, 128), jnp.float32)
    loads[6].wait()
    row_events(0)
    prepare_table(0, 40)
    row_events(1)
    prepare_table(40, 80)
    col_near(0, 0)
    prepare_table(80, 120)
    row_far(0)
    row_far(1)
    prepare_table(120, 160)
    col_near(0, 1)
    prepare_table(160, 200)
    col_near(0, 2)
    col_far(0, 0)
    prepare_table(200, 240)
    col_near(1, 0)
    col_near(0, 3)
    prepare_table(240, 280)
    col_far(0, 1)
    col_near(1, 1)
    prepare_table(280, 316)
    col_far(0, 2)
    col_near(1, 2)
    col_far(0, 3)
    to_smem.wait()
    loads[5].wait()
    twin_all(0)
    translate(0, 0, 4)
    col_near(1, 3)
    col_far(1, 0)
    translate(0, 4, 8)
    col_far(1, 1)
    translate(0, 8, 12)
    col_far(1, 2)
    translate(0, 12, 16)
    col_far(1, 3)
    take_out(0)
    edge_out[0] = pack_low([incpad[1, odd, c, 8 * i : 8 * i + 8, :] for odd, c, i in GROUPS])
    edge_out[1] = pack_high([incpad[4, odd, c, 8 * i : 8 * i + 8, :] for odd, c, i in GROUPS])
    edges = [
        pltpu.make_async_remote_copy(
            src_ref=edge_out.at[side],
            dst_ref=edge_in.at[side],
            send_sem=edge_send.at[side],
            recv_sem=edge_recv.at[side],
            device_id={"sample": there},
            device_id_type=MESH,
        )
        for side, there in ((0, z_low), (1, z_high))
    ]
    for edge in edges:
        edge.start()
    twin_all(1)
    translate(1, 0, 16)
    take_out(1)
    for edge in edges:
        edge.wait_recv()
    for g, (odd, c, i) in enumerate(GROUPS):
        incpad[5, odd, c, 8 * i : 8 * i + 8, :] = as_high_halo(edge_in[0], g)
        incpad[0, odd, c, 8 * i : 8 * i + 8, :] = as_low_halo(edge_in[1], g)
    loads[7].wait()

    def disaggregate(p, _):
        rows = pl.ds(pl.multiple_of(8 * p, 8), 8)
        moved = []
        for odd in range(2):
            real, imag = (
                jnp.concatenate(
                    [jnp.broadcast_to(incpad[blk, odd, c, pl.ds(p, 1), :], (8, 128)) for blk in range(6)], 1
                )
                for c in range(2)
            )
            cosine, sine = cs[0, odd], cs[1, odd]
            moved.append((cosine * real + sine * imag, cosine * imag - sine * real))
        for c in range(2):
            total = clv[c, rows, :]
            for tap in range(TAPS):
                v = wb[0, tap] * moved[0][c] + wb[1, tap] * moved[1][c]
                shift = (tap - 2) % 768
                v = pltpu.roll(v, shift, 1) if shift else v
                total = total + v[:, 128:640]
            out1[c, rows, :] = total
        return 0

    lax.fori_loop(0, PAR, disaggregate, 0)

    for halo in halos:
        halo.wait_send()
    for edge in edges:
        edge.wait_send()
    sent_all(0)
    sent_all(1)


def local(child_pattern, child_local, interp_weight, child_phase, translator, partners, operator_id, list_len):
    operators = translator.shape[0]
    folded = translator.reshape(operators, 2, 8, 128).transpose(0, 2, 1, 3).reshape(operators, 16, 128)
    f32 = jnp.float32
    any_spec = pl.BlockSpec(memory_space=pl.ANY)
    vmem_spec = pl.BlockSpec(memory_space=pltpu.VMEM)
    return pl.pallas_call(
        kernel,
        out_shape=(
            jax.ShapeDtypeStruct((2, PAR, 1024), f32),
            jax.ShapeDtypeStruct((2, 128, 512), f32),
        ),
        in_specs=[any_spec] * 8,
        out_specs=(vmem_spec, vmem_spec),
        scratch_shapes=[
            pltpu.VMEM((512, 8, 128), f32),
            pltpu.VMEM((512, 8, 128), f32),
            pltpu.VMEM((320, 16, 128), f32),
            pltpu.VMEM((320, 16, 128), f32),
            pltpu.VMEM((128, 128), f32),
            pltpu.VMEM((128, 128), f32),
            pltpu.VMEM((316, 16, 128), f32),
            pltpu.VMEM((2, 128, 768), f32),
            pltpu.VMEM((2, 128, 512), f32),
            pltpu.VMEM((6, 1024), f32),
            pltpu.VMEM((8, 1024), f32),
            pltpu.VMEM((2, 8, 768), f32),
            pltpu.VMEM((2, 8, 768), f32),
            pltpu.VMEM((2, 2, 8, 768), f32),
            pltpu.VMEM((2, 6, 8, 768), f32),
            pltpu.VMEM((4, 2, 2, 16, 128), f32),
            pltpu.VMEM((6, 2, 2, 16, 128), f32),
            pltpu.VMEM((16, 64), jnp.int32),
            pltpu.VMEM((16, 64), jnp.int32),
            pltpu.SMEM((16, 64), jnp.int32),
            pltpu.SMEM((16, 64), jnp.int32),
            pltpu.SMEM((512,), jnp.int32),
            pltpu.VMEM((2, 2, 8, 128), f32),
            pltpu.VMEM((2, 2, 8, 128), f32),
            pltpu.VMEM((2, 8, 128), f32),
            pltpu.VMEM((2, 8, 128), f32),
            pltpu.SemaphoreType.DMA((8,)),
            pltpu.SemaphoreType.DMA,
            pltpu.SemaphoreType.DMA((2,)),
            pltpu.SemaphoreType.DMA((2, 3)),
            pltpu.SemaphoreType.DMA((2, 4, 3)),
            pltpu.SemaphoreType.DMA((2,)),
            pltpu.SemaphoreType.DMA((2,)),
            pltpu.SemaphoreType.DMA((2,)),
            pltpu.SemaphoreType.DMA((2,)),
            pltpu.SemaphoreType.DMA((2,)),
        ],
        compiler_params=pltpu.CompilerParams(
            collective_id=0, has_side_effects=True, vmem_limit_bytes=48 * 1024 * 1024
        ),
    )(child_pattern, child_local, interp_weight, child_phase, folded, partners, operator_id, list_len)


def solution(mesh):
    placed = (
        P(None, "cluster", "sample"),
        P(None, "cluster", "sample"),
        P(None, "sample"),
        P(None, "sample"),
        P(None, None, "sample"),
        P(),
        P(),
        P(),
    )
    return jax.shard_map(
        local,
        mesh=mesh,
        in_specs=placed,
        out_specs=(P(None, "cluster", "sample"), P(None, "cluster", "sample")),
        check_vma=False,
    )
```

```python
import functools

import jax
import jax.numpy as jnp
from jax import lax
from jax.experimental import pallas as pl
from jax.experimental.pallas import tpu as pltpu
from jax.sharding import PartitionSpec as P

TAPS = 6
CHILDREN = 8
PAR = 16
NT = 316
LMAX = 64
MESH = pl.DeviceIdType.MESH
CHUNK_OF = {0: (0, 0), 3: (0, 2), 2: (1, 0), 1: (1, 2)}


def lanes():
    return lax.broadcasted_iota(jnp.int32, (8, 128), 1)


def subs():
    return lax.broadcasted_iota(jnp.int32, (8, 128), 0)


def take(v, index):
    return jnp.take_along_axis(v, index, axis=1)


def split_pairs(v0, v1):
    lane = lanes()
    even = (2 * lane) % 128
    return tuple(
        jnp.where(lane < 64, take(v0, even + odd), take(v1, even + odd)) for odd in (0, 1)
    )


def join_pairs(e, o):
    lane = lanes()
    made = []
    for half in (0, 64):
        at = half + lane // 2
        made.append(jnp.where(lane % 2 == 0, take(e, at), take(o, at)))
    return made


def pack_low(groups):
    lane = lanes()
    total = jnp.zeros((8, 128), jnp.float32)
    for g, v in enumerate(groups):
        total = jnp.where(lane // 4 == g, pltpu.roll(v, 4 * g, 1) if g else v, total)
    return total


def pack_high(groups):
    lane = lanes()
    total = jnp.zeros((8, 128), jnp.float32)
    for g, v in enumerate(groups):
        shift = (4 * g + 4) % 128
        total = jnp.where(lane // 4 == g, pltpu.roll(v, shift, 1) if shift else v, total)
    return total


def as_high_halo(packed, g):
    return pltpu.roll(packed, (128 - 4 * g) % 128, 1) if g else packed


def as_low_halo(packed, g):
    shift = (128 - (4 * g + 4)) % 128
    return pltpu.roll(packed, shift, 1) if shift else packed


def kernel(
    cp, cl, w, ph, t, part, oper, length,
    out0, out1,
    p_0, p_1, ab_0, ab_1, inc_0, inc_1, tv, xpad, clv, wv, phv, wpad, phpad, cs, wb, agg, incpad,
    opv, opm, pidx, oidx, lens,
    halo_out, halo_in, edge_out, edge_in,
    load_sem, index_sem, send_sem, row_sem, col_sem, twin_sem, halo_send, halo_recv, edge_send, edge_recv,
):
    gathered, tables, incoming = (p_0, p_1), (ab_0, ab_1), (inc_0, inc_1)
    me = lax.axis_index("cluster")
    z = lax.axis_index("sample")
    core = me % 2
    y = (me // 2) % 4
    x = me // 8
    step_a = 8 - 6 * core
    step_b = 2 + 6 * core
    at_a = x * (1 - core) + y * core
    at_b = y * (1 - core) + x * core
    twin = me + 1 - 2 * core

    def dev(da, db):
        return step_a * ((at_a + da + 4) % 4) + step_b * ((at_b + db + 4) % 4) + core

    z_low = (z + 31) % 32
    z_high = (z + 1) % 32

    first_col = pl.multiple_of(128 * (me // 8), 128)
    own_col = PAR * (me % 8)
    loads = [
        pltpu.make_async_copy(w, wv, load_sem.at[0]),
        pltpu.make_async_copy(ph, phv, load_sem.at[1]),
        pltpu.make_async_copy(cp, xpad.at[:, :, pl.ds(128, 512)], load_sem.at[2]),
        pltpu.make_async_copy(oper.at[:, pl.ds(first_col, 128)], opv, load_sem.at[3]),
        pltpu.make_async_copy(length, lens, load_sem.at[4]),
        pltpu.make_async_copy(part.at[:, pl.ds(first_col, 128)], pidx, load_sem.at[5]),
        pltpu.make_async_copy(t, tv, load_sem.at[6]),
        pltpu.make_async_copy(cl, clv, load_sem.at[7]),
    ]
    for load in loads:
        load.start()

    barrier = pltpu.get_barrier_semaphore()
    for there in (dev(1, 0), dev(-1, 0), dev(0, 1), dev(0, -1), twin):
        pl.semaphore_signal(barrier, inc=1, device_id={"cluster": there}, device_id_type=MESH)
    for there in (z_low, z_high):
        pl.semaphore_signal(barrier, inc=1, device_id={"sample": there}, device_id_type=MESH)

    loads[0].wait()
    loads[1].wait()
    for b in range(4):
        main = pl.ds(128 * (b + 1), 128)
        halves = []
        for k in (2 * b, 2 * b + 1):
            halves.append(
                jnp.concatenate([wv[:, 128 * k : 128 * (k + 1)], jnp.zeros((2, 128), jnp.float32)], 0)
            )
        for odd, v in enumerate(split_pairs(*halves)):
            wpad[odd, :, main] = v
        for odd, v in enumerate(
            split_pairs(
                phv[:, 256 * b : 256 * b + 128],
                phv[:, 256 * b + 128 : 256 * b + 256],
            )
        ):
            phpad[odd, :, main] = v

    loads[2].wait()

    def ends(block, packer):
        here = pl.ds(128 * (block + 1), 128)
        children = [xpad[c, 8 * p : 8 * p + 8, here] for c in range(2) for p in range(PAR)]
        others = [wpad[0, :, here], wpad[1, :, here], phpad[0, :, here], phpad[1, :, here]]
        return packer(children), packer(others)

    halo_out[0, 0], halo_out[0, 1] = ends(0, pack_low)
    halo_out[1, 0], halo_out[1, 1] = ends(3, pack_high)
    pl.semaphore_wait(barrier, 7)
    halos = [
        pltpu.make_async_remote_copy(
            src_ref=halo_out.at[side],
            dst_ref=halo_in.at[side],
            send_sem=halo_send.at[side],
            recv_sem=halo_recv.at[side],
            device_id={"sample": there},
            device_id_type=MESH,
        )
        for side, there in ((0, z_low), (1, z_high))
    ]
    for halo in halos:
        halo.start()

    for odd in range(2):
        cs[0, odd, :, 128:640] = jnp.cos(phpad[odd, :, 128:640])
        cs[1, odd, :, 128:640] = jnp.sin(phpad[odd, :, 128:640])

    def broadcast_weights(blocks):
        for odd in range(2):
            for tap in range(TAPS):
                for blk in blocks:
                    here = pl.ds(128 * blk, 128)
                    wb[odd, tap, :, here] = jnp.broadcast_to(wpad[odd, tap : tap + 1, here], (8, 128))

    broadcast_weights(range(1, 5))

    def aggregate(b):
        main = pl.ds(128 * (b + 1), 128)
        weight = [[wb[odd, tap, :, main] for tap in range(TAPS)] for odd in range(2)]
        cosine = [cs[0, odd, :, main] for odd in range(2)]
        sine = [cs[1, odd, :, main] for odd in range(2)]

        def one(p, _):
            rows = pl.ds(pl.multiple_of(8 * p, 8), 8)
            up = []
            for c in range(2):
                wide = xpad[c, rows, pl.ds(128 * b, 384)]
                window = [wide[:, 126 + tap : 254 + tap] for tap in range(TAPS)]
                up.append(
                    [sum(weight[odd][tap] * window[tap] for tap in range(TAPS)) for odd in range(2)]
                )
            for odd in range(2):
                real = cosine[odd] * up[0][odd] - sine[odd] * up[1][odd]
                imag = cosine[odd] * up[1][odd] + sine[odd] * up[0][odd]
                agg[b, odd, 0, pl.ds(p, 1), :] = jnp.sum(real, axis=0, keepdims=True)
                agg[b, odd, 1, pl.ds(p, 1), :] = jnp.sum(imag, axis=0, keepdims=True)
            return 0

        lax.fori_loop(0, PAR, one, 0, unroll=4)
        chunk, place = CHUNK_OF[b]
        for c in range(2):
            for i in range(2):
                pieces = [agg[b, odd, c, 8 * i : 8 * i + 8, :] for odd in range(2)]
                for half, v in enumerate(join_pairs(*pieces)):
                    gathered[chunk][pl.ds(me * PAR + 8 * i, 8), 2 * (place + half) + c, :] = v

    def block(h, d):
        return gathered[h].at[pl.ds(d * PAR, PAR)]

    def send(h, d, target, arrived):
        pltpu.make_async_remote_copy(
            src_ref=block(h, d),
            dst_ref=block(h, d),
            send_sem=send_sem.at[h],
            recv_sem=arrived,
            device_id={"cluster": target},
            device_id_type=MESH,
        ).start()

    def arrive(h, d, arrived):
        pltpu.make_async_remote_copy(
            src_ref=block(h, d),
            dst_ref=block(h, d),
            send_sem=send_sem.at[h],
            recv_sem=arrived,
            device_id={"cluster": twin},
            device_id_type=MESH,
        ).wait_recv()

    def give_twin(h, d):
        send(h, d, twin, twin_sem.at[h])

    OFF = (0, -1, 1, 2)

    def spread_b(h, g):
        d = dev(OFF[g], 0)
        send(h, d, dev(0, 1), col_sem.at[h, g, 0])
        send(h, d, dev(0, -1), col_sem.at[h, g, 1])

    def own(h):
        send(h, me, dev(1, 0), row_sem.at[h, 0])
        send(h, me, dev(-1, 0), row_sem.at[h, 1])
        spread_b(h, 0)
        give_twin(h, me)

    def row_events(h):
        for side, da in ((0, -1), (1, 1)):
            arrive(h, dev(da, 0), row_sem.at[h, side])
            if side == h:
                send(h, dev(da, 0), dev(-da, 0), row_sem.at[h, 2])
            spread_b(h, 1 + side)
            give_twin(h, dev(da, 0))

    def row_far(h):
        arrive(h, dev(2, 0), row_sem.at[h, 2])
        spread_b(h, 3)
        give_twin(h, dev(2, 0))

    def col_near(h, g):
        for side, db in ((0, -1), (1, 1)):
            d = dev(OFF[g], db)
            arrive(h, d, col_sem.at[h, g, side])
            if side == h:
                send(h, d, dev(0, -db), col_sem.at[h, g, 2])
            give_twin(h, d)

    def col_far(h, g):
        d = dev(OFF[g], 2)
        arrive(h, d, col_sem.at[h, g, 2])
        give_twin(h, d)

    def twin_all(h):
        half = gathered[h].at[pl.ds(0, 256)]
        pltpu.make_async_remote_copy(
            src_ref=half, dst_ref=half, send_sem=send_sem.at[h], recv_sem=twin_sem.at[h],
            device_id={"cluster": twin}, device_id_type=MESH,
        ).wait_recv()

    def sent_all(h):
        most = gathered[h].at[pl.ds(0, 31 * PAR)]
        pltpu.make_async_remote_copy(
            src_ref=most, dst_ref=most, send_sem=send_sem.at[h], recv_sem=twin_sem.at[h],
            device_id={"cluster": twin}, device_id_type=MESH,
        ).wait_send()

    def prepare_table(start, stop):
        def one(o, _):
            sub = subs()
            t0 = tv[o, 0:8, :]
            t1 = tv[o, 8:16, :]
            for ab, v in ((ab_0, jnp.where(sub < 4, t0, t1)), (ab_1, jnp.where(sub < 4, t1, t0))):
                ab[o, 0:8, :] = jnp.where(sub % 2 == 0, v, pltpu.roll(v, 1, 0))
                ab[o, 8:16, :] = jnp.where(sub % 2 == 0, pltpu.roll(v, 7, 0), -v)
            return 0

        lax.fori_loop(start, stop, one, 0)

    def translate(h, start, stop):
        def one(q, _):
            first = [jnp.zeros((8, 128), jnp.float32) for _ in range(2)]
            second = [jnp.zeros((8, 128), jnp.float32) for _ in range(2)]
            for slot in range(LMAX):
                source = gathered[h][pidx[slot, own_col + q]]
                table = tables[h][oidx[slot, own_col + q]]
                first[slot % 2] += table[0:8] * source
                second[slot % 2] += table[8:16] * source
            cross = second[0] + second[1]
            swapped = jnp.where(subs() % 2 == 0, pltpu.roll(cross, 7, 0), pltpu.roll(cross, 1, 0))
            incoming[h][pl.ds(pl.multiple_of(8 * q, 8), 8), :] = first[0] + first[1] + swapped
            return 0

        lax.fori_loop(start, stop, one, 0)

    def take_out(h):
        for b in range(4):
            chunk, place = CHUNK_OF[b]
            if chunk != h:
                continue
            for c in range(2):
                for i in range(2):
                    pieces = []
                    for half in range(2):
                        v = incoming[h][pl.ds(64 * i + 2 * (place + half) + c, 8, stride=8), :]
                        out0[c, 8 * i : 8 * i + 8, pl.ds(128 * (2 * b + half), 128)] = v
                        pieces.append(v)
                    for odd, v in enumerate(split_pairs(*pieces)):
                        incpad[b + 1, odd, c, 8 * i : 8 * i + 8, :] = v

    GROUPS = [(odd, c, i) for odd in range(2) for c in range(2) for i in range(2)]

    aggregate(2)
    aggregate(1)
    own(1)
    loads[3].wait()
    loads[4].wait()
    loads[5].wait()
    live = jnp.zeros((1, 128), jnp.int32)
    column = lax.broadcasted_iota(jnp.int32, (1, 128), 1)
    for i in range(PAR):
        live = jnp.where(column == own_col + i, lens[me * PAR + i], live)
    slot = lax.broadcasted_iota(jnp.int32, (LMAX, 128), 0)
    opm[...] = jnp.where(slot < live, opv[...], NT)
    to_smem = [
        pltpu.make_async_copy(opm, oidx, index_sem.at[0]),
    ]
    for copy in to_smem:
        copy.start()

    for halo in halos:
        halo.wait_recv()
    for c in range(2):
        for p in range(PAR):
            g = PAR * c + p
            xpad[c, 8 * p : 8 * p + 8, 640:768] = as_high_halo(halo_in[0, 0], g)
            xpad[c, 8 * p : 8 * p + 8, 0:128] = as_low_halo(halo_in[1, 0], g)
    aggregate(0)
    aggregate(3)
    own(0)

    for g, padded in enumerate((wpad, wpad, phpad, phpad)):
        padded[g % 2, :, 640:768] = as_high_halo(halo_in[0, 1], g)
        padded[g % 2, :, 0:128] = as_low_halo(halo_in[1, 1], g)
    for odd in range(2):
        for here in (slice(0, 128), slice(640, 768)):
            cs[0, odd, :, here] = jnp.cos(phpad[odd, :, here])
            cs[1, odd, :, here] = jnp.sin(phpad[odd, :, here])
    broadcast_weights((0, 5))

    for ab in tables:
        ab[NT] = jnp.zeros((16, 128), jnp.float32)
    loads[6].wait()
    row_events(0)
    prepare_table(0, 40)
    row_events(1)
    prepare_table(40, 80)
    col_near(0, 0)
    prepare_table(80, 120)
    row_far(0)
    row_far(1)
    prepare_table(120, 160)
    col_near(0, 1)
    prepare_table(160, 200)
    col_near(0, 2)
    col_far(0, 0)
    prepare_table(200, 240)
    col_near(1, 0)
    col_near(0, 3)
    prepare_table(240, 280)
    col_far(0, 1)
    col_near(1, 1)
    prepare_table(280, 316)
    col_far(0, 2)
    col_near(1, 2)
    col_far(0, 3)
    for copy in to_smem:
        copy.wait()
    twin_all(0)
    translate(0, 0, 4)
    col_near(1, 3)
    col_far(1, 0)
    translate(0, 4, 8)
    col_far(1, 1)
    translate(0, 8, 12)
    col_far(1, 2)
    translate(0, 12, 16)
    col_far(1, 3)
    take_out(0)
    edge_out[0] = pack_low([incpad[1, odd, c, 8 * i : 8 * i + 8, :] for odd, c, i in GROUPS])
    edge_out[1] = pack_high([incpad[4, odd, c, 8 * i : 8 * i + 8, :] for odd, c, i in GROUPS])
    edges = [
        pltpu.make_async_remote_copy(
            src_ref=edge_out.at[side],
            dst_ref=edge_in.at[side],
            send_sem=edge_send.at[side],
            recv_sem=edge_recv.at[side],
            device_id={"sample": there},
            device_id_type=MESH,
        )
        for side, there in ((0, z_low), (1, z_high))
    ]
    for edge in edges:
        edge.start()
    twin_all(1)
    translate(1, 0, 16)
    take_out(1)
    for edge in edges:
        edge.wait_recv()
    for g, (odd, c, i) in enumerate(GROUPS):
        incpad[5, odd, c, 8 * i : 8 * i + 8, :] = as_high_halo(edge_in[0], g)
        incpad[0, odd, c, 8 * i : 8 * i + 8, :] = as_low_halo(edge_in[1], g)
    loads[7].wait()

    def disaggregate(p, _):
        rows = pl.ds(pl.multiple_of(8 * p, 8), 8)
        moved = []
        for odd in range(2):
            real, imag = (
                jnp.concatenate(
                    [jnp.broadcast_to(incpad[blk, odd, c, pl.ds(p, 1), :], (8, 128)) for blk in range(6)], 1
                )
                for c in range(2)
            )
            cosine, sine = cs[0, odd], cs[1, odd]
            moved.append((cosine * real + sine * imag, cosine * imag - sine * real))
        for c in range(2):
            total = clv[c, rows, :]
            for tap in range(TAPS):
                v = wb[0, tap] * moved[0][c] + wb[1, tap] * moved[1][c]
                shift = (tap - 2) % 768
                v = pltpu.roll(v, shift, 1) if shift else v
                total = total + v[:, 128:640]
            out1[c, rows, :] = total
        return 0

    lax.fori_loop(0, PAR, disaggregate, 0, unroll=2)

    for halo in halos:
        halo.wait_send()
    for edge in edges:
        edge.wait_send()
    sent_all(0)
    sent_all(1)


def local(child_pattern, child_local, interp_weight, child_phase, translator, partners, operator_id, list_len):
    operators = translator.shape[0]
    folded = translator.reshape(operators, 2, 8, 128).transpose(0, 2, 1, 3).reshape(operators, 16, 128)
    f32 = jnp.float32
    any_spec = pl.BlockSpec(memory_space=pl.ANY)
    vmem_spec = pl.BlockSpec(memory_space=pltpu.VMEM)
    return pl.pallas_call(
        kernel,
        out_shape=(
            jax.ShapeDtypeStruct((2, PAR, 1024), f32),
            jax.ShapeDtypeStruct((2, 128, 512), f32),
        ),
        in_specs=[any_spec] * 8,
        out_specs=(vmem_spec, vmem_spec),
        scratch_shapes=[
            pltpu.VMEM((512, 8, 128), f32),
            pltpu.VMEM((512, 8, 128), f32),
            pltpu.VMEM((320, 16, 128), f32),
            pltpu.VMEM((320, 16, 128), f32),
            pltpu.VMEM((128, 128), f32),
            pltpu.VMEM((128, 128), f32),
            pltpu.VMEM((316, 16, 128), f32),
            pltpu.VMEM((2, 128, 768), f32),
            pltpu.VMEM((2, 128, 512), f32),
            pltpu.VMEM((6, 1024), f32),
            pltpu.VMEM((8, 1024), f32),
            pltpu.VMEM((2, 8, 768), f32),
            pltpu.VMEM((2, 8, 768), f32),
            pltpu.VMEM((2, 2, 8, 768), f32),
            pltpu.VMEM((2, 6, 8, 768), f32),
            pltpu.VMEM((4, 2, 2, 16, 128), f32),
            pltpu.VMEM((6, 2, 2, 16, 128), f32),
            pltpu.VMEM((64, 128), jnp.int32),
            pltpu.VMEM((64, 128), jnp.int32),
            pltpu.SMEM((64, 128), jnp.int32),
            pltpu.SMEM((64, 128), jnp.int32),
            pltpu.SMEM((512,), jnp.int32),
            pltpu.VMEM((2, 2, 8, 128), f32),
            pltpu.VMEM((2, 2, 8, 128), f32),
            pltpu.VMEM((2, 8, 128), f32),
            pltpu.VMEM((2, 8, 128), f32),
            pltpu.SemaphoreType.DMA((8,)),
            pltpu.SemaphoreType.DMA((2,)),
            pltpu.SemaphoreType.DMA((2,)),
            pltpu.SemaphoreType.DMA((2, 3)),
            pltpu.SemaphoreType.DMA((2, 4, 3)),
            pltpu.SemaphoreType.DMA((2,)),
            pltpu.SemaphoreType.DMA((2,)),
            pltpu.SemaphoreType.DMA((2,)),
            pltpu.SemaphoreType.DMA((2,)),
            pltpu.SemaphoreType.DMA((2,)),
        ],
        compiler_params=pltpu.CompilerParams(
            collective_id=0, has_side_effects=True, vmem_limit_bytes=56 * 1024 * 1024
        ),
    )(child_pattern, child_local, interp_weight, child_phase, folded, partners.T, operator_id.T, list_len)


def solution(mesh):
    placed = (
        P(None, "cluster", "sample"),
        P(None, "cluster", "sample"),
        P(None, "sample"),
        P(None, "sample"),
        P(None, None, "sample"),
        P(),
        P(),
        P(),
    )
    return jax.shard_map(
        local,
        mesh=mesh,
        in_specs=placed,
        out_specs=(P(None, "cluster", "sample"), P(None, "cluster", "sample")),
        check_vma=False,
    )
```

```python
import functools

import jax
import jax.numpy as jnp
from jax import lax
from jax.experimental import pallas as pl
from jax.experimental.pallas import tpu as pltpu
from jax.sharding import PartitionSpec as P

TAPS = 6
CHILDREN = 8
PAR = 16
NT = 316
LMAX = 64
MESH = pl.DeviceIdType.MESH
CHUNK_OF = {0: (0, 0), 3: (0, 2), 2: (1, 0), 1: (1, 2)}


def lanes():
    return lax.broadcasted_iota(jnp.int32, (8, 128), 1)


def subs():
    return lax.broadcasted_iota(jnp.int32, (8, 128), 0)


def take(v, index):
    return jnp.take_along_axis(v, index, axis=1)


def split_pairs(v0, v1):
    lane = lanes()
    even = (2 * lane) % 128
    return tuple(
        jnp.where(lane < 64, take(v0, even + odd), take(v1, even + odd)) for odd in (0, 1)
    )


def join_pairs(e, o):
    lane = lanes()
    made = []
    for half in (0, 64):
        at = half + lane // 2
        made.append(jnp.where(lane % 2 == 0, take(e, at), take(o, at)))
    return made


def pack_low(groups):
    lane = lanes()
    total = jnp.zeros((8, 128), jnp.float32)
    for g, v in enumerate(groups):
        total = jnp.where(lane // 4 == g, pltpu.roll(v, 4 * g, 1) if g else v, total)
    return total


def pack_high(groups):
    lane = lanes()
    total = jnp.zeros((8, 128), jnp.float32)
    for g, v in enumerate(groups):
        shift = (4 * g + 4) % 128
        total = jnp.where(lane // 4 == g, pltpu.roll(v, shift, 1) if shift else v, total)
    return total


def as_high_halo(packed, g):
    return pltpu.roll(packed, (128 - 4 * g) % 128, 1) if g else packed


def as_low_halo(packed, g):
    shift = (128 - (4 * g + 4)) % 128
    return pltpu.roll(packed, shift, 1) if shift else packed


def kernel(
    cp, cl, w, ph, t, part, oper, length,
    out0, out1,
    p_0, p_1, ab_0, ab_1, inc_0, inc_1, tv, xpad, clv, wv, phv, wpad, phpad, cs, wb, agg, incpad,
    opv, opm, pidx, oidx, lens,
    halo_out, halo_in, edge_out, edge_in,
    load_sem, index_sem, send_sem, row_sem, col_sem, twin_sem, halo_send, halo_recv, edge_send, edge_recv,
):
    gathered, tables, incoming = (p_0, p_1), (ab_0, ab_1), (inc_0, inc_1)
    me = lax.axis_index("cluster")
    z = lax.axis_index("sample")
    core = me % 2
    y = (me // 2) % 4
    x = me // 8
    step_a = 8 - 6 * core
    step_b = 2 + 6 * core
    at_a = x * (1 - core) + y * core
    at_b = y * (1 - core) + x * core
    twin = me + 1 - 2 * core

    def dev(da, db):
        return step_a * ((at_a + da + 4) % 4) + step_b * ((at_b + db + 4) % 4) + core

    z_low = (z + 31) % 32
    z_high = (z + 1) % 32

    first_col = pl.multiple_of(128 * (me // 8), 128)
    own_col = PAR * (me % 8)
    loads = [
        pltpu.make_async_copy(w, wv, load_sem.at[0]),
        pltpu.make_async_copy(ph, phv, load_sem.at[1]),
        pltpu.make_async_copy(cp, xpad.at[:, :, pl.ds(128, 512)], load_sem.at[2]),
        pltpu.make_async_copy(oper.at[:, pl.ds(first_col, 128)], opv, load_sem.at[3]),
        pltpu.make_async_copy(length, lens, load_sem.at[4]),
        pltpu.make_async_copy(part.at[:, pl.ds(first_col, 128)], pidx, load_sem.at[5]),
        pltpu.make_async_copy(t, tv, load_sem.at[6]),
        pltpu.make_async_copy(cl, clv, load_sem.at[7]),
    ]
    for load in loads:
        load.start()

    barrier = pltpu.get_barrier_semaphore()
    for there in (dev(1, 0), dev(-1, 0), dev(0, 1), dev(0, -1), twin):
        pl.semaphore_signal(barrier, inc=1, device_id={"cluster": there}, device_id_type=MESH)
    for there in (z_low, z_high):
        pl.semaphore_signal(barrier, inc=1, device_id={"sample": there}, device_id_type=MESH)

    loads[0].wait()
    loads[1].wait()
    for b in range(4):
        main = pl.ds(128 * (b + 1), 128)
        halves = []
        for k in (2 * b, 2 * b + 1):
            halves.append(
                jnp.concatenate([wv[:, 128 * k : 128 * (k + 1)], jnp.zeros((2, 128), jnp.float32)], 0)
            )
        for odd, v in enumerate(split_pairs(*halves)):
            wpad[odd, :, main] = v
        for odd, v in enumerate(
            split_pairs(
                phv[:, 256 * b : 256 * b + 128],
                phv[:, 256 * b + 128 : 256 * b + 256],
            )
        ):
            phpad[odd, :, main] = v

    loads[2].wait()

    def ends(block, packer):
        here = pl.ds(128 * (block + 1), 128)
        children = [xpad[c, 8 * p : 8 * p + 8, here] for c in range(2) for p in range(PAR)]
        others = [wpad[0, :, here], wpad[1, :, here], phpad[0, :, here], phpad[1, :, here]]
        return packer(children), packer(others)

    halo_out[0, 0], halo_out[0, 1] = ends(0, pack_low)
    halo_out[1, 0], halo_out[1, 1] = ends(3, pack_high)
    pl.semaphore_wait(barrier, 7)
    halos = [
        pltpu.make_async_remote_copy(
            src_ref=halo_out.at[side],
            dst_ref=halo_in.at[side],
            send_sem=halo_send.at[side],
            recv_sem=halo_recv.at[side],
            device_id={"sample": there},
            device_id_type=MESH,
        )
        for side, there in ((0, z_low), (1, z_high))
    ]
    for halo in halos:
        halo.start()

    for odd in range(2):
        cs[0, odd, :, 128:640] = jnp.cos(phpad[odd, :, 128:640])
        cs[1, odd, :, 128:640] = jnp.sin(phpad[odd, :, 128:640])

    def broadcast_weights(blocks):
        for odd in range(2):
            for tap in range(TAPS):
                for blk in blocks:
                    here = pl.ds(128 * blk, 128)
                    wb[odd, tap, :, here] = jnp.broadcast_to(wpad[odd, tap : tap + 1, here], (8, 128))

    broadcast_weights(range(1, 5))

    def aggregate(b):
        main = pl.ds(128 * (b + 1), 128)
        weight = [[wb[odd, tap, :, main] for tap in range(TAPS)] for odd in range(2)]
        cosine = [cs[0, odd, :, main] for odd in range(2)]
        sine = [cs[1, odd, :, main] for odd in range(2)]

        def one(p, _):
            rows = pl.ds(pl.multiple_of(8 * p, 8), 8)
            up = []
            for c in range(2):
                wide = xpad[c, rows, pl.ds(128 * b, 384)]
                window = [wide[:, 126 + tap : 254 + tap] for tap in range(TAPS)]
                up.append(
                    [sum(weight[odd][tap] * window[tap] for tap in range(TAPS)) for odd in range(2)]
                )
            for odd in range(2):
                real = cosine[odd] * up[0][odd] - sine[odd] * up[1][odd]
                imag = cosine[odd] * up[1][odd] + sine[odd] * up[0][odd]
                agg[b, odd, 0, pl.ds(p, 1), :] = jnp.sum(real, axis=0, keepdims=True)
                agg[b, odd, 1, pl.ds(p, 1), :] = jnp.sum(imag, axis=0, keepdims=True)
            return 0

        lax.fori_loop(0, PAR, one, 0, unroll=4)
        chunk, place = CHUNK_OF[b]
        for c in range(2):
            for i in range(2):
                pieces = [agg[b, odd, c, 8 * i : 8 * i + 8, :] for odd in range(2)]
                for half, v in enumerate(join_pairs(*pieces)):
                    gathered[chunk][pl.ds(me * PAR + 8 * i, 8), 2 * (place + half) + c, :] = v

    def block(h, d):
        return gathered[h].at[pl.ds(d * PAR, PAR)]

    def send(h, d, target, arrived):
        pltpu.make_async_remote_copy(
            src_ref=block(h, d),
            dst_ref=block(h, d),
            send_sem=send_sem.at[h],
            recv_sem=arrived,
            device_id={"cluster": target},
            device_id_type=MESH,
        ).start()

    def arrive(h, d, arrived):
        pltpu.make_async_remote_copy(
            src_ref=block(h, d),
            dst_ref=block(h, d),
            send_sem=send_sem.at[h],
            recv_sem=arrived,
            device_id={"cluster": twin},
            device_id_type=MESH,
        ).wait_recv()

    def give_twin(h, d):
        send(h, d, twin, twin_sem.at[h])

    OFF = (0, -1, 1, 2)

    def spread_b(h, g):
        d = dev(OFF[g], 0)
        send(h, d, dev(0, 1), col_sem.at[h, g, 0])
        send(h, d, dev(0, -1), col_sem.at[h, g, 1])

    def own(h):
        send(h, me, dev(1, 0), row_sem.at[h, 0])
        send(h, me, dev(-1, 0), row_sem.at[h, 1])
        spread_b(h, 0)
        give_twin(h, me)

    def row_events(h):
        for side, da in ((0, -1), (1, 1)):
            arrive(h, dev(da, 0), row_sem.at[h, side])
            if side == h:
                send(h, dev(da, 0), dev(-da, 0), row_sem.at[h, 2])
            spread_b(h, 1 + side)
            give_twin(h, dev(da, 0))

    def row_far(h):
        arrive(h, dev(2, 0), row_sem.at[h, 2])
        spread_b(h, 3)
        give_twin(h, dev(2, 0))

    def col_near(h, g):
        for side, db in ((0, -1), (1, 1)):
            d = dev(OFF[g], db)
            arrive(h, d, col_sem.at[h, g, side])
            if side == h:
                send(h, d, dev(0, -db), col_sem.at[h, g, 2])
            give_twin(h, d)

    def col_far(h, g):
        d = dev(OFF[g], 2)
        arrive(h, d, col_sem.at[h, g, 2])
        give_twin(h, d)

    def twin_all(h):
        half = gathered[h].at[pl.ds(0, 256)]
        pltpu.make_async_remote_copy(
            src_ref=half, dst_ref=half, send_sem=send_sem.at[h], recv_sem=twin_sem.at[h],
            device_id={"cluster": twin}, device_id_type=MESH,
        ).wait_recv()

    def sent_all(h):
        most = gathered[h].at[pl.ds(0, 31 * PAR)]
        pltpu.make_async_remote_copy(
            src_ref=most, dst_ref=most, send_sem=send_sem.at[h], recv_sem=twin_sem.at[h],
            device_id={"cluster": twin}, device_id_type=MESH,
        ).wait_send()

    def prepare_table(start, stop):
        def one(o, _):
            sub = subs()
            t0 = tv[o, 0:8, :]
            t1 = tv[o, 8:16, :]
            for ab, v in ((ab_0, jnp.where(sub < 4, t0, t1)), (ab_1, jnp.where(sub < 4, t1, t0))):
                ab[o, 0:8, :] = jnp.where(sub % 2 == 0, v, pltpu.roll(v, 1, 0))
                ab[o, 8:16, :] = jnp.where(sub % 2 == 0, pltpu.roll(v, 7, 0), -v)
            return 0

        lax.fori_loop(start, stop, one, 0)

    def translate(h, start, stop):
        def one(q, _):
            first = [jnp.zeros((8, 128), jnp.float32) for _ in range(2)]
            second = [jnp.zeros((8, 128), jnp.float32) for _ in range(2)]
            for slot in range(LMAX):
                source = gathered[h][pidx[slot, own_col + q]]
                table = tables[h][oidx[slot, own_col + q]]
                first[slot % 2] += table[0:8] * source
                second[slot % 2] += table[8:16] * source
            cross = second[0] + second[1]
            swapped = jnp.where(subs() % 2 == 0, pltpu.roll(cross, 7, 0), pltpu.roll(cross, 1, 0))
            incoming[h][pl.ds(pl.multiple_of(8 * q, 8), 8), :] = first[0] + first[1] + swapped
            return 0

        lax.fori_loop(start, stop, one, 0)

    def take_out(h):
        for b in range(4):
            chunk, place = CHUNK_OF[b]
            if chunk != h:
                continue
            for c in range(2):
                for i in range(2):
                    pieces = []
                    for half in range(2):
                        v = incoming[h][pl.ds(64 * i + 2 * (place + half) + c, 8, stride=8), :]
                        out0[c, 8 * i : 8 * i + 8, pl.ds(128 * (2 * b + half), 128)] = v
                        pieces.append(v)
                    for odd, v in enumerate(split_pairs(*pieces)):
                        incpad[b + 1, odd, c, 8 * i : 8 * i + 8, :] = v

    GROUPS = [(odd, c, i) for odd in range(2) for c in range(2) for i in range(2)]

    aggregate(2)
    aggregate(1)
    own(1)
    loads[3].wait()
    loads[4].wait()
    loads[5].wait()
    live = jnp.zeros((1, 128), jnp.int32)
    column = lax.broadcasted_iota(jnp.int32, (1, 128), 1)
    for i in range(PAR):
        live = jnp.where(column == own_col + i, lens[me * PAR + i], live)
    slot = lax.broadcasted_iota(jnp.int32, (LMAX, 128), 0)
    opm[...] = jnp.where(slot < live, opv[...], NT)
    to_smem = [
        pltpu.make_async_copy(opm, oidx, index_sem.at[0]),
    ]
    for copy in to_smem:
        copy.start()

    for halo in halos:
        halo.wait_recv()
    for c in range(2):
        for p in range(PAR):
            g = PAR * c + p
            xpad[c, 8 * p : 8 * p + 8, 640:768] = as_high_halo(halo_in[0, 0], g)
            xpad[c, 8 * p : 8 * p + 8, 0:128] = as_low_halo(halo_in[1, 0], g)
    aggregate(0)
    aggregate(3)
    own(0)

    for g, padded in enumerate((wpad, wpad, phpad, phpad)):
        padded[g % 2, :, 640:768] = as_high_halo(halo_in[0, 1], g)
        padded[g % 2, :, 0:128] = as_low_halo(halo_in[1, 1], g)
    for odd in range(2):
        for here in (slice(0, 128), slice(640, 768)):
            cs[0, odd, :, here] = jnp.cos(phpad[odd, :, here])
            cs[1, odd, :, here] = jnp.sin(phpad[odd, :, here])
    broadcast_weights((0, 5))

    for ab in tables:
        ab[NT] = jnp.zeros((16, 128), jnp.float32)
    loads[6].wait()
    row_events(0)
    prepare_table(0, 40)
    row_events(1)
    prepare_table(40, 80)
    col_near(0, 0)
    prepare_table(80, 120)
    row_far(0)
    row_far(1)
    prepare_table(120, 160)
    col_near(0, 1)
    prepare_table(160, 200)
    col_near(0, 2)
    col_far(0, 0)
    prepare_table(200, 240)
    col_near(1, 0)
    col_near(0, 3)
    prepare_table(240, 280)
    col_far(0, 1)
    col_near(1, 1)
    prepare_table(280, 316)
    col_far(0, 2)
    col_near(1, 2)
    col_far(0, 3)
    for copy in to_smem:
        copy.wait()
    twin_all(0)
    translate(0, 0, 4)
    col_near(1, 3)
    col_far(1, 0)
    translate(0, 4, 8)
    col_far(1, 1)
    translate(0, 8, 12)
    col_far(1, 2)
    translate(0, 12, 16)
    col_far(1, 3)
    take_out(0)
    edge_out[0] = pack_low([incpad[1, odd, c, 8 * i : 8 * i + 8, :] for odd, c, i in GROUPS])
    edge_out[1] = pack_high([incpad[4, odd, c, 8 * i : 8 * i + 8, :] for odd, c, i in GROUPS])
    edges = [
        pltpu.make_async_remote_copy(
            src_ref=edge_out.at[side],
            dst_ref=edge_in.at[side],
            send_sem=edge_send.at[side],
            recv_sem=edge_recv.at[side],
            device_id={"sample": there},
            device_id_type=MESH,
        )
        for side, there in ((0, z_low), (1, z_high))
    ]
    for edge in edges:
        edge.start()
    twin_all(1)
    translate(1, 0, 16)
    take_out(1)
    for edge in edges:
        edge.wait_recv()
    for g, (odd, c, i) in enumerate(GROUPS):
        incpad[5, odd, c, 8 * i : 8 * i + 8, :] = as_high_halo(edge_in[0], g)
        incpad[0, odd, c, 8 * i : 8 * i + 8, :] = as_low_halo(edge_in[1], g)
    loads[7].wait()

    def disaggregate(p, _):
        rows = pl.ds(pl.multiple_of(8 * p, 8), 8)
        moved = []
        for odd in range(2):
            real, imag = (
                jnp.concatenate(
                    [jnp.broadcast_to(incpad[blk, odd, c, pl.ds(p, 1), :], (8, 128)) for blk in range(6)], 1
                )
                for c in range(2)
            )
            cosine, sine = cs[0, odd], cs[1, odd]
            moved.append((cosine * real + sine * imag, cosine * imag - sine * real))
        for c in range(2):
            total = clv[c, rows, :]
            for tap in range(TAPS):
                v = wb[0, tap] * moved[0][c] + wb[1, tap] * moved[1][c]
                shift = (tap - 2) % 768
                v = pltpu.roll(v, shift, 1) if shift else v
                total = total + v[:, 128:640]
            out1[c, rows, :] = total
        return 0

    lax.fori_loop(0, PAR, disaggregate, 0, unroll=2)

    for halo in halos:
        halo.wait_send()
    for edge in edges:
        edge.wait_send()
    sent_all(0)
    sent_all(1)


def hand_over(parents, children, out0, out1, held0, held1, sem):
    pieces = []
    for c in range(2):
        pieces.append((parents.at[c], held0.at[c], out0.at[c]))
        for i in range(4):
            rows = pl.ds(32 * i, 32)
            pieces.append((children.at[c, rows], held1.at[c, rows], out1.at[c, rows]))
    reads = [pltpu.make_async_copy(a, b, sem.at[0, k]) for k, (a, b, _) in enumerate(pieces)]
    writes = [pltpu.make_async_copy(b, c, sem.at[1, k]) for k, (_, b, c) in enumerate(pieces)]
    for read in reads:
        read.start()
    for read, write in zip(reads, writes):
        read.wait()
        write.start()
    for write in writes:
        write.wait()


def local(child_pattern, child_local, interp_weight, child_phase, translator, partners, operator_id, list_len):
    operators = translator.shape[0]
    folded = translator.reshape(operators, 2, 8, 128).transpose(0, 2, 1, 3).reshape(operators, 16, 128)
    f32 = jnp.float32
    any_spec = pl.BlockSpec(memory_space=pl.ANY)
    vmem_spec = pl.BlockSpec(memory_space=pltpu.VMEM)
    parents, children = pl.pallas_call(
        kernel,
        out_shape=(
            jax.ShapeDtypeStruct((2, PAR, 1024), f32),
            jax.ShapeDtypeStruct((2, 128, 512), f32),
        ),
        in_specs=[any_spec] * 8,
        out_specs=(vmem_spec, vmem_spec),
        scratch_shapes=[
            pltpu.VMEM((512, 8, 128), f32),
            pltpu.VMEM((512, 8, 128), f32),
            pltpu.VMEM((320, 16, 128), f32),
            pltpu.VMEM((320, 16, 128), f32),
            pltpu.VMEM((128, 128), f32),
            pltpu.VMEM((128, 128), f32),
            pltpu.VMEM((316, 16, 128), f32),
            pltpu.VMEM((2, 128, 768), f32),
            pltpu.VMEM((2, 128, 512), f32),
            pltpu.VMEM((6, 1024), f32),
            pltpu.VMEM((8, 1024), f32),
            pltpu.VMEM((2, 8, 768), f32),
            pltpu.VMEM((2, 8, 768), f32),
            pltpu.VMEM((2, 2, 8, 768), f32),
            pltpu.VMEM((2, 6, 8, 768), f32),
            pltpu.VMEM((4, 2, 2, 16, 128), f32),
            pltpu.VMEM((6, 2, 2, 16, 128), f32),
            pltpu.VMEM((64, 128), jnp.int32),
            pltpu.VMEM((64, 128), jnp.int32),
            pltpu.SMEM((64, 128), jnp.int32),
            pltpu.SMEM((64, 128), jnp.int32),
            pltpu.SMEM((512,), jnp.int32),
            pltpu.VMEM((2, 2, 8, 128), f32),
            pltpu.VMEM((2, 2, 8, 128), f32),
            pltpu.VMEM((2, 8, 128), f32),
            pltpu.VMEM((2, 8, 128), f32),
            pltpu.SemaphoreType.DMA((8,)),
            pltpu.SemaphoreType.DMA((2,)),
            pltpu.SemaphoreType.DMA((2,)),
            pltpu.SemaphoreType.DMA((2, 3)),
            pltpu.SemaphoreType.DMA((2, 4, 3)),
            pltpu.SemaphoreType.DMA((2,)),
            pltpu.SemaphoreType.DMA((2,)),
            pltpu.SemaphoreType.DMA((2,)),
            pltpu.SemaphoreType.DMA((2,)),
            pltpu.SemaphoreType.DMA((2,)),
        ],
        compiler_params=pltpu.CompilerParams(
            collective_id=0, has_side_effects=True, vmem_limit_bytes=56 * 1024 * 1024
        ),
    )(child_pattern, child_local, interp_weight, child_phase, folded, partners.T, operator_id.T, list_len)
    return pl.pallas_call(
        hand_over,
        out_shape=(
            jax.ShapeDtypeStruct((2, PAR, 1024), f32),
            jax.ShapeDtypeStruct((2, 128, 512), f32),
        ),
        in_specs=[any_spec] * 2,
        out_specs=(any_spec, any_spec),
        scratch_shapes=[
            pltpu.VMEM((2, PAR, 1024), f32),
            pltpu.VMEM((2, 128, 512), f32),
            pltpu.SemaphoreType.DMA((2, 10)),
        ],
        compiler_params=pltpu.CompilerParams(vmem_limit_bytes=56 * 1024 * 1024),
    )(parents, children)


def solution(mesh):
    placed = (
        P(None, "cluster", "sample"),
        P(None, "cluster", "sample"),
        P(None, "sample"),
        P(None, "sample"),
        P(None, None, "sample"),
        P(),
        P(),
        P(),
    )
    return jax.shard_map(
        local,
        mesh=mesh,
        in_specs=placed,
        out_specs=(P(None, "cluster", "sample"), P(None, "cluster", "sample")),
        check_vma=False,
    )
```

```python
import functools

import jax
import jax.numpy as jnp
from jax import lax
from jax.experimental import pallas as pl
from jax.experimental.pallas import tpu as pltpu
from jax.sharding import PartitionSpec as P

TAPS = 6
CHILDREN = 8
PAR = 16
NT = 316
LMAX = 64
MESH = pl.DeviceIdType.MESH
CHUNK_OF = {0: (0, 0), 3: (0, 2), 2: (1, 0), 1: (1, 2)}


def lanes():
    return lax.broadcasted_iota(jnp.int32, (8, 128), 1)


def subs():
    return lax.broadcasted_iota(jnp.int32, (8, 128), 0)


def take(v, index):
    return jnp.take_along_axis(v, index, axis=1)


def split_pairs(v0, v1):
    lane = lanes()
    even = (2 * lane) % 128
    return tuple(
        jnp.where(lane < 64, take(v0, even + odd), take(v1, even + odd)) for odd in (0, 1)
    )


def join_pairs(e, o):
    lane = lanes()
    made = []
    for half in (0, 64):
        at = half + lane // 2
        made.append(jnp.where(lane % 2 == 0, take(e, at), take(o, at)))
    return made


def pack_low(groups):
    lane = lanes()
    total = jnp.zeros((8, 128), jnp.float32)
    for g, v in enumerate(groups):
        total = jnp.where(lane // 4 == g, pltpu.roll(v, 4 * g, 1) if g else v, total)
    return total


def pack_high(groups):
    lane = lanes()
    total = jnp.zeros((8, 128), jnp.float32)
    for g, v in enumerate(groups):
        shift = (4 * g + 4) % 128
        total = jnp.where(lane // 4 == g, pltpu.roll(v, shift, 1) if shift else v, total)
    return total


def as_high_halo(packed, g):
    return pltpu.roll(packed, (128 - 4 * g) % 128, 1) if g else packed


def as_low_halo(packed, g):
    shift = (128 - (4 * g + 4)) % 128
    return pltpu.roll(packed, shift, 1) if shift else packed


def kernel(
    cp, cl, w, ph, t, part, oper, length,
    out0, out1,
    p_0, p_1, ab_0, ab_1, inc_0, inc_1, tv, xpad, clv, wv, phv, wpad, phpad, cs, wb, agg, incpad,
    opv, opm, pidx, oidx, lens,
    halo_out, halo_in, edge_out, edge_in,
    load_sem, index_sem, send_sem, row_sem, col_sem, twin_sem, halo_send, halo_recv, edge_send, edge_recv,
):
    gathered, tables, incoming = (p_0, p_1), (ab_0, ab_1), (inc_0, inc_1)
    me = lax.axis_index("cluster")
    z = lax.axis_index("sample")
    core = me % 2
    y = (me // 2) % 4
    x = me // 8
    step_a = 8 - 6 * core
    step_b = 2 + 6 * core
    at_a = x * (1 - core) + y * core
    at_b = y * (1 - core) + x * core
    twin = me + 1 - 2 * core

    def dev(da, db):
        return step_a * ((at_a + da + 4) % 4) + step_b * ((at_b + db + 4) % 4) + core

    z_low = (z + 31) % 32
    z_high = (z + 1) % 32

    first_col = pl.multiple_of(128 * (me // 8), 128)
    own_col = PAR * (me % 8)
    loads = [
        pltpu.make_async_copy(w, wv, load_sem.at[0]),
        pltpu.make_async_copy(ph, phv, load_sem.at[1]),
        pltpu.make_async_copy(cp, xpad.at[:, :, pl.ds(128, 512)], load_sem.at[2]),
        pltpu.make_async_copy(oper.at[:, pl.ds(first_col, 128)], opv, load_sem.at[3]),
        pltpu.make_async_copy(length, lens, load_sem.at[4]),
        pltpu.make_async_copy(part.at[:, pl.ds(first_col, 128)], pidx, load_sem.at[5]),
        pltpu.make_async_copy(t, tv, load_sem.at[6]),
        pltpu.make_async_copy(cl, clv, load_sem.at[7]),
    ]
    for load in loads:
        load.start()

    barrier = pltpu.get_barrier_semaphore()
    for there in (dev(1, 0), dev(-1, 0), dev(0, 1), dev(0, -1), twin):
        pl.semaphore_signal(barrier, inc=1, device_id={"cluster": there}, device_id_type=MESH)
    for there in (z_low, z_high):
        pl.semaphore_signal(barrier, inc=1, device_id={"sample": there}, device_id_type=MESH)

    loads[0].wait()
    loads[1].wait()
    for b in range(4):
        main = pl.ds(128 * (b + 1), 128)
        halves = []
        for k in (2 * b, 2 * b + 1):
            halves.append(
                jnp.concatenate([wv[:, 128 * k : 128 * (k + 1)], jnp.zeros((2, 128), jnp.float32)], 0)
            )
        for odd, v in enumerate(split_pairs(*halves)):
            wpad[odd, :, main] = v
        for odd, v in enumerate(
            split_pairs(
                phv[:, 256 * b : 256 * b + 128],
                phv[:, 256 * b + 128 : 256 * b + 256],
            )
        ):
            phpad[odd, :, main] = v

    loads[2].wait()

    def ends(block, packer):
        here = pl.ds(128 * (block + 1), 128)
        children = [xpad[c, 8 * p : 8 * p + 8, here] for c in range(2) for p in range(PAR)]
        others = [wpad[0, :, here], wpad[1, :, here], phpad[0, :, here], phpad[1, :, here]]
        return packer(children), packer(others)

    halo_out[0, 0], halo_out[0, 1] = ends(0, pack_low)
    halo_out[1, 0], halo_out[1, 1] = ends(3, pack_high)
    pl.semaphore_wait(barrier, 7)
    halos = [
        pltpu.make_async_remote_copy(
            src_ref=halo_out.at[side],
            dst_ref=halo_in.at[side],
            send_sem=halo_send.at[side],
            recv_sem=halo_recv.at[side],
            device_id={"sample": there},
            device_id_type=MESH,
        )
        for side, there in ((0, z_low), (1, z_high))
    ]
    for halo in halos:
        halo.start()

    for odd in range(2):
        cs[0, odd, :, 128:640] = jnp.cos(phpad[odd, :, 128:640])
        cs[1, odd, :, 128:640] = jnp.sin(phpad[odd, :, 128:640])

    def broadcast_weights(blocks):
        for odd in range(2):
            for tap in range(TAPS):
                for blk in blocks:
                    here = pl.ds(128 * blk, 128)
                    wb[odd, tap, :, here] = jnp.broadcast_to(wpad[odd, tap : tap + 1, here], (8, 128))

    broadcast_weights(range(1, 5))

    def aggregate(b):
        main = pl.ds(128 * (b + 1), 128)
        weight = [[wb[odd, tap, :, main] for tap in range(TAPS)] for odd in range(2)]
        cosine = [cs[0, odd, :, main] for odd in range(2)]
        sine = [cs[1, odd, :, main] for odd in range(2)]

        def one(p, _):
            rows = pl.ds(pl.multiple_of(8 * p, 8), 8)
            up = []
            for c in range(2):
                wide = xpad[c, rows, pl.ds(128 * b, 384)]
                window = [wide[:, 126 + tap : 254 + tap] for tap in range(TAPS)]
                up.append(
                    [sum(weight[odd][tap] * window[tap] for tap in range(TAPS)) for odd in range(2)]
                )
            for odd in range(2):
                real = cosine[odd] * up[0][odd] - sine[odd] * up[1][odd]
                imag = cosine[odd] * up[1][odd] + sine[odd] * up[0][odd]
                agg[b, odd, 0, pl.ds(p, 1), :] = jnp.sum(real, axis=0, keepdims=True)
                agg[b, odd, 1, pl.ds(p, 1), :] = jnp.sum(imag, axis=0, keepdims=True)
            return 0

        lax.fori_loop(0, PAR, one, 0, unroll=True)
        chunk, place = CHUNK_OF[b]
        for c in range(2):
            for i in range(2):
                pieces = [agg[b, odd, c, 8 * i : 8 * i + 8, :] for odd in range(2)]
                for half, v in enumerate(join_pairs(*pieces)):
                    gathered[chunk][pl.ds(me * PAR + 8 * i, 8), 2 * (place + half) + c, :] = v

    def block(h, d):
        return gathered[h].at[pl.ds(d * PAR, PAR)]

    def send(h, d, target, arrived):
        pltpu.make_async_remote_copy(
            src_ref=block(h, d),
            dst_ref=block(h, d),
            send_sem=send_sem.at[h],
            recv_sem=arrived,
            device_id={"cluster": target},
            device_id_type=MESH,
        ).start()

    def arrive(h, d, arrived):
        pltpu.make_async_remote_copy(
            src_ref=block(h, d),
            dst_ref=block(h, d),
            send_sem=send_sem.at[h],
            recv_sem=arrived,
            device_id={"cluster": twin},
            device_id_type=MESH,
        ).wait_recv()

    def give_twin(h, d):
        send(h, d, twin, twin_sem.at[h])

    OFF = (0, -1, 1, 2)

    def spread_b(h, g):
        d = dev(OFF[g], 0)
        send(h, d, dev(0, 1), col_sem.at[h, g, 0])
        send(h, d, dev(0, -1), col_sem.at[h, g, 1])

    def own(h):
        send(h, me, dev(1, 0), row_sem.at[h, 0])
        send(h, me, dev(-1, 0), row_sem.at[h, 1])
        spread_b(h, 0)
        give_twin(h, me)

    def row_events(h):
        for side, da in ((0, -1), (1, 1)):
            arrive(h, dev(da, 0), row_sem.at[h, side])
            if side == h:
                send(h, dev(da, 0), dev(-da, 0), row_sem.at[h, 2])
            spread_b(h, 1 + side)
            give_twin(h, dev(da, 0))

    def row_far(h):
        arrive(h, dev(2, 0), row_sem.at[h, 2])
        spread_b(h, 3)
        give_twin(h, dev(2, 0))

    def col_near(h, g):
        for side, db in ((0, -1), (1, 1)):
            d = dev(OFF[g], db)
            arrive(h, d, col_sem.at[h, g, side])
            if side == h:
                send(h, d, dev(0, -db), col_sem.at[h, g, 2])
            give_twin(h, d)

    def col_far(h, g):
        d = dev(OFF[g], 2)
        arrive(h, d, col_sem.at[h, g, 2])
        give_twin(h, d)

    def twin_all(h):
        half = gathered[h].at[pl.ds(0, 256)]
        pltpu.make_async_remote_copy(
            src_ref=half, dst_ref=half, send_sem=send_sem.at[h], recv_sem=twin_sem.at[h],
            device_id={"cluster": twin}, device_id_type=MESH,
        ).wait_recv()

    def sent_all(h):
        most = gathered[h].at[pl.ds(0, 31 * PAR)]
        pltpu.make_async_remote_copy(
            src_ref=most, dst_ref=most, send_sem=send_sem.at[h], recv_sem=twin_sem.at[h],
            device_id={"cluster": twin}, device_id_type=MESH,
        ).wait_send()

    def prepare_table(start, stop):
        def one(o, _):
            sub = subs()
            t0 = tv[o, 0:8, :]
            t1 = tv[o, 8:16, :]
            for ab, v in ((ab_0, jnp.where(sub < 4, t0, t1)), (ab_1, jnp.where(sub < 4, t1, t0))):
                ab[o, 0:8, :] = jnp.where(sub % 2 == 0, v, pltpu.roll(v, 1, 0))
                ab[o, 8:16, :] = jnp.where(sub % 2 == 0, pltpu.roll(v, 7, 0), -v)
            return 0

        lax.fori_loop(start, stop, one, 0)

    def translate(h, start, stop):
        def one(q, _):
            first = [jnp.zeros((8, 128), jnp.float32) for _ in range(2)]
            second = [jnp.zeros((8, 128), jnp.float32) for _ in range(2)]
            for slot in range(LMAX):
                source = gathered[h][pidx[slot, own_col + q]]
                table = tables[h][oidx[slot, own_col + q]]
                first[slot % 2] += table[0:8] * source
                second[slot % 2] += table[8:16] * source
            cross = second[0] + second[1]
            swapped = jnp.where(subs() % 2 == 0, pltpu.roll(cross, 7, 0), pltpu.roll(cross, 1, 0))
            incoming[h][pl.ds(pl.multiple_of(8 * q, 8), 8), :] = first[0] + first[1] + swapped
            return 0

        lax.fori_loop(start, stop, one, 0)

    def take_out(h):
        for b in range(4):
            chunk, place = CHUNK_OF[b]
            if chunk != h:
                continue
            for c in range(2):
                for i in range(2):
                    pieces = []
                    for half in range(2):
                        v = incoming[h][pl.ds(64 * i + 2 * (place + half) + c, 8, stride=8), :]
                        out0[c, 8 * i : 8 * i + 8, pl.ds(128 * (2 * b + half), 128)] = v
                        pieces.append(v)
                    for odd, v in enumerate(split_pairs(*pieces)):
                        incpad[b + 1, odd, c, 8 * i : 8 * i + 8, :] = v

    GROUPS = [(odd, c, i) for odd in range(2) for c in range(2) for i in range(2)]

    aggregate(2)
    aggregate(1)
    own(1)
    loads[3].wait()
    loads[4].wait()
    loads[5].wait()
    live = jnp.zeros((1, 128), jnp.int32)
    column = lax.broadcasted_iota(jnp.int32, (1, 128), 1)
    for i in range(PAR):
        live = jnp.where(column == own_col + i, lens[me * PAR + i], live)
    slot = lax.broadcasted_iota(jnp.int32, (LMAX, 128), 0)
    opm[...] = jnp.where(slot < live, opv[...], NT)
    to_smem = [
        pltpu.make_async_copy(opm, oidx, index_sem.at[0]),
    ]
    for copy in to_smem:
        copy.start()

    for halo in halos:
        halo.wait_recv()
    for c in range(2):
        for p in range(PAR):
            g = PAR * c + p
            xpad[c, 8 * p : 8 * p + 8, 640:768] = as_high_halo(halo_in[0, 0], g)
            xpad[c, 8 * p : 8 * p + 8, 0:128] = as_low_halo(halo_in[1, 0], g)
    aggregate(0)
    aggregate(3)
    own(0)

    for g, padded in enumerate((wpad, wpad, phpad, phpad)):
        padded[g % 2, :, 640:768] = as_high_halo(halo_in[0, 1], g)
        padded[g % 2, :, 0:128] = as_low_halo(halo_in[1, 1], g)
    for odd in range(2):
        for here in (slice(0, 128), slice(640, 768)):
            cs[0, odd, :, here] = jnp.cos(phpad[odd, :, here])
            cs[1, odd, :, here] = jnp.sin(phpad[odd, :, here])
    broadcast_weights((0, 5))

    for ab in tables:
        ab[NT] = jnp.zeros((16, 128), jnp.float32)
    loads[6].wait()
    row_events(0)
    prepare_table(0, 40)
    row_events(1)
    prepare_table(40, 80)
    col_near(0, 0)
    prepare_table(80, 120)
    row_far(0)
    row_far(1)
    prepare_table(120, 160)
    col_near(0, 1)
    prepare_table(160, 200)
    col_near(0, 2)
    col_far(0, 0)
    prepare_table(200, 240)
    col_near(1, 0)
    col_near(0, 3)
    prepare_table(240, 280)
    col_far(0, 1)
    col_near(1, 1)
    prepare_table(280, 316)
    col_far(0, 2)
    col_near(1, 2)
    col_far(0, 3)
    for copy in to_smem:
        copy.wait()
    twin_all(0)
    translate(0, 0, 4)
    col_near(1, 3)
    col_far(1, 0)
    translate(0, 4, 8)
    col_far(1, 1)
    translate(0, 8, 12)
    col_far(1, 2)
    translate(0, 12, 16)
    col_far(1, 3)
    take_out(0)
    edge_out[0] = pack_low([incpad[1, odd, c, 8 * i : 8 * i + 8, :] for odd, c, i in GROUPS])
    edge_out[1] = pack_high([incpad[4, odd, c, 8 * i : 8 * i + 8, :] for odd, c, i in GROUPS])
    edges = [
        pltpu.make_async_remote_copy(
            src_ref=edge_out.at[side],
            dst_ref=edge_in.at[side],
            send_sem=edge_send.at[side],
            recv_sem=edge_recv.at[side],
            device_id={"sample": there},
            device_id_type=MESH,
        )
        for side, there in ((0, z_low), (1, z_high))
    ]
    for edge in edges:
        edge.start()
    twin_all(1)
    translate(1, 0, 16)
    take_out(1)
    for edge in edges:
        edge.wait_recv()
    for g, (odd, c, i) in enumerate(GROUPS):
        incpad[5, odd, c, 8 * i : 8 * i + 8, :] = as_high_halo(edge_in[0], g)
        incpad[0, odd, c, 8 * i : 8 * i + 8, :] = as_low_halo(edge_in[1], g)
    loads[7].wait()

    def disaggregate(p, _):
        rows = pl.ds(pl.multiple_of(8 * p, 8), 8)
        moved = []
        for odd in range(2):
            real, imag = (
                jnp.concatenate(
                    [jnp.broadcast_to(incpad[blk, odd, c, pl.ds(p, 1), :], (8, 128)) for blk in range(6)], 1
                )
                for c in range(2)
            )
            cosine, sine = cs[0, odd], cs[1, odd]
            moved.append((cosine * real + sine * imag, cosine * imag - sine * real))
        for c in range(2):
            total = clv[c, rows, :]
            for tap in range(TAPS):
                v = wb[0, tap] * moved[0][c] + wb[1, tap] * moved[1][c]
                shift = (tap - 2) % 768
                v = pltpu.roll(v, shift, 1) if shift else v
                total = total + v[:, 128:640]
            out1[c, rows, :] = total
        return 0

    lax.fori_loop(0, PAR, disaggregate, 0, unroll=2)

    for halo in halos:
        halo.wait_send()
    for edge in edges:
        edge.wait_send()
    sent_all(0)
    sent_all(1)


def hand_over(parents, children, out0, out1, held0, held1, sem):
    pieces = []
    for c in range(2):
        pieces.append((parents.at[c], held0.at[c], out0.at[c]))
        for i in range(4):
            rows = pl.ds(32 * i, 32)
            pieces.append((children.at[c, rows], held1.at[c, rows], out1.at[c, rows]))
    reads = [pltpu.make_async_copy(a, b, sem.at[0, k]) for k, (a, b, _) in enumerate(pieces)]
    writes = [pltpu.make_async_copy(b, c, sem.at[1, k]) for k, (_, b, c) in enumerate(pieces)]
    for read in reads:
        read.start()
    for read, write in zip(reads, writes):
        read.wait()
        write.start()
    for write in writes:
        write.wait()


def local(child_pattern, child_local, interp_weight, child_phase, translator, partners, operator_id, list_len):
    operators = translator.shape[0]
    folded = translator.reshape(operators, 2, 8, 128).transpose(0, 2, 1, 3).reshape(operators, 16, 128)
    f32 = jnp.float32
    any_spec = pl.BlockSpec(memory_space=pl.ANY)
    vmem_spec = pl.BlockSpec(memory_space=pltpu.VMEM)
    parents, children = pl.pallas_call(
        kernel,
        out_shape=(
            jax.ShapeDtypeStruct((2, PAR, 1024), f32),
            jax.ShapeDtypeStruct((2, 128, 512), f32),
        ),
        in_specs=[any_spec] * 8,
        out_specs=(vmem_spec, vmem_spec),
        scratch_shapes=[
            pltpu.VMEM((512, 8, 128), f32),
            pltpu.VMEM((512, 8, 128), f32),
            pltpu.VMEM((320, 16, 128), f32),
            pltpu.VMEM((320, 16, 128), f32),
            pltpu.VMEM((128, 128), f32),
            pltpu.VMEM((128, 128), f32),
            pltpu.VMEM((316, 16, 128), f32),
            pltpu.VMEM((2, 128, 768), f32),
            pltpu.VMEM((2, 128, 512), f32),
            pltpu.VMEM((6, 1024), f32),
            pltpu.VMEM((8, 1024), f32),
            pltpu.VMEM((2, 8, 768), f32),
            pltpu.VMEM((2, 8, 768), f32),
            pltpu.VMEM((2, 2, 8, 768), f32),
            pltpu.VMEM((2, 6, 8, 768), f32),
            pltpu.VMEM((4, 2, 2, 16, 128), f32),
            pltpu.VMEM((6, 2, 2, 16, 128), f32),
            pltpu.VMEM((64, 128), jnp.int32),
            pltpu.VMEM((64, 128), jnp.int32),
            pltpu.SMEM((64, 128), jnp.int32),
            pltpu.SMEM((64, 128), jnp.int32),
            pltpu.SMEM((512,), jnp.int32),
            pltpu.VMEM((2, 2, 8, 128), f32),
            pltpu.VMEM((2, 2, 8, 128), f32),
            pltpu.VMEM((2, 8, 128), f32),
            pltpu.VMEM((2, 8, 128), f32),
            pltpu.SemaphoreType.DMA((8,)),
            pltpu.SemaphoreType.DMA((2,)),
            pltpu.SemaphoreType.DMA((2,)),
            pltpu.SemaphoreType.DMA((2, 3)),
            pltpu.SemaphoreType.DMA((2, 4, 3)),
            pltpu.SemaphoreType.DMA((2,)),
            pltpu.SemaphoreType.DMA((2,)),
            pltpu.SemaphoreType.DMA((2,)),
            pltpu.SemaphoreType.DMA((2,)),
            pltpu.SemaphoreType.DMA((2,)),
        ],
        compiler_params=pltpu.CompilerParams(
            collective_id=0, has_side_effects=True, vmem_limit_bytes=56 * 1024 * 1024
        ),
    )(child_pattern, child_local, interp_weight, child_phase, folded, partners.T, operator_id.T, list_len)
    return pl.pallas_call(
        hand_over,
        out_shape=(
            jax.ShapeDtypeStruct((2, PAR, 1024), f32),
            jax.ShapeDtypeStruct((2, 128, 512), f32),
        ),
        in_specs=[any_spec] * 2,
        out_specs=(any_spec, any_spec),
        scratch_shapes=[
            pltpu.VMEM((2, PAR, 1024), f32),
            pltpu.VMEM((2, 128, 512), f32),
            pltpu.SemaphoreType.DMA((2, 10)),
        ],
        compiler_params=pltpu.CompilerParams(vmem_limit_bytes=56 * 1024 * 1024),
    )(parents, children)


def solution(mesh):
    placed = (
        P(None, "cluster", "sample"),
        P(None, "cluster", "sample"),
        P(None, "sample"),
        P(None, "sample"),
        P(None, None, "sample"),
        P(),
        P(),
        P(),
    )
    return jax.shard_map(
        local,
        mesh=mesh,
        in_specs=placed,
        out_specs=(P(None, "cluster", "sample"), P(None, "cluster", "sample")),
        check_vma=False,
    )
```
